1024 devices in a mesh: dp: 128 (over x_lo, z, core), group: 8 (over x_hi, y).
Axes of the slice: x: 4 (x_hi: 2, x_lo: 2; x = x_hi * 2 + x_lo), y: 4, z: 32, core: 2. Of those that a mesh axis runs over, the one named last changes fastest.
Arguments:
- picture_vectors: bfloat16 [8, 16384, 1152], P('group', 'dp'), may hold values from -6 to 6
- caption_vectors: bfloat16 [8, 16384, 1152], P('group', 'dp'), may hold values from -6 to 6
- matched_caption_slot: int32 [8, 128, 128], P('group', 'dp'), may hold values from 0 to 127, each once within a row
- sharpness_coefficient: float32 [1], replicated, may hold values from 2 to 8
- affinity_offset: float32 [1], replicated, may hold values from -3 to -1
Outputs:
- picture_derivative: float32 [8, 16384, 1152], P('group', 'dp')
- text_grad: float32 [8, 16384, 1152], P('group', 'dp')
The draws below stay inside these ranges and needn't reach their ends.
Inputs may be any that keep to these rules, and one draw needn't show every extreme that they name: `matched_caption_slot`: each row of one device is a permutation of 0 .. 127.
All inputs are finite; a program needn't handle non-finite values.
Results may differ from the reference program's by a relative error of at most 0.0085.
Values may be sent and summed in bfloat16 or wider, within the bound.
No kernel may reach another device: no remote copies, remote signals or barrier semaphores. Data moves between devices by JAX's collectives and lax.ppermute only.
A program may use at most 32 MiB of HBM per device.

```python
import math
import jax
import jax.numpy as jnp
import numpy as np
from jax import lax

E = 1152
P_SIZE = 128
ROUNDS = 8
BD = 16384
N_DP = 128
N_GROUP = 8


def block_scale(own_key, dims, shards, low, top_value):
    factor_of, own = 1.0, jax.random.fold_in(own_key, 6)
    for axis_at, parts in shards:
        draws = jnp.exp(jax.random.uniform(jax.random.fold_in(own, axis_at), (parts,), jnp.float32, low / len(shards), top_value / len(shards)))
        factor_of = factor_of * jnp.repeat(draws, dims[axis_at] // parts).reshape([-1 if axis == axis_at else 1 for axis in range(len(dims))])
    return factor_of


def scatter_about(key, extent, spread, limit, split=(), kind=jnp.bfloat16):
    drawn = spread * jax.random.normal(key, extent, jnp.float32)
    if split:
        drawn = drawn * block_scale(key, extent, split, -0.22, 0.18)
    return jnp.clip(drawn, -limit, limit).astype(kind)


def setup_inputs(seed: int = 0) -> dict:
    keys = jax.random.split(jax.random.key(seed), 6)
    return {
        "picture_vectors": scatter_about(keys[0], (N_GROUP, BD, E), 1.0, 6.0, ((0, 8), (1, 128))),
        "caption_vectors": scatter_about(keys[1], (N_GROUP, BD, E), 1.0, 6.0, ((0, 8), (1, 128))),
        "matched_caption_slot": jax.vmap(lambda own: jax.random.permutation(own, P_SIZE))(jax.random.split(keys[2], N_GROUP * N_DP)).reshape((N_GROUP, N_DP, P_SIZE)).astype(jnp.int32),
        "sharpness_coefficient": jnp.clip(jnp.exp(jax.random.uniform(keys[3], (1,), jnp.float32, math.log(2.0), math.log(8.0))), 2.0, 8.0),
        "affinity_offset": jnp.clip(jax.random.uniform(keys[4], (1,), jnp.float32, -3.0, -1.0), -3.0, -1.0),
    }


def normalize(values):
    wide = values.astype(jnp.float32)
    inverse_norm_factor = lax.rsqrt(lax.optimization_barrier(jnp.sum(wide * wide, axis=-1, keepdims=True)) + 1e-06)
    return (wide * inverse_norm_factor, inverse_norm_factor)

def reference(picture_vectors, caption_vectors, matched_caption_slot, sharpness_coefficient, affinity_offset):
    xn, inv_x = normalize(picture_vectors.reshape(N_GROUP, N_DP, P_SIZE, E))
    yn, inv_y = normalize(caption_vectors.reshape(N_GROUP, N_DP, P_SIZE, E))
    xb = xn.astype(jnp.bfloat16).astype(jnp.float32)
    yb = yn.astype(jnp.bfloat16).astype(jnp.float32)
    similarity_multiplier = sharpness_coefficient[0]
    shift = affinity_offset[0]
    columns = jnp.arange(P_SIZE, dtype=jnp.int32)
    positive = matched_caption_slot[:, :, :, None] == columns[None, None, None, :]
    image_embedding_gradient = jnp.zeros((N_GROUP, N_DP, P_SIZE, E), jnp.float32)
    grad_y = jnp.zeros((N_GROUP, N_DP, P_SIZE, E), jnp.float32)
    for step in range(ROUNDS):
        lower_bits_mask = step % 4
        high_mask = step // 4
        partner_group_sequence = np.arange(N_GROUP) ^ high_mask
        block_order = np.arange(N_DP) ^ lower_bits_mask
        partner = yb[partner_group_sequence][:, block_order]
        logits = similarity_multiplier * jnp.einsum('gdpe,gdqe->gdpq', xb, partner) + shift
        if step == 0:
            sign = jnp.where(positive, 1.0, -1.0).astype(jnp.float32)
        else:
            sign = -jnp.ones_like(logits)
        coef = (-similarity_multiplier * sign * jax.nn.sigmoid(-sign * logits)).astype(jnp.bfloat16).astype(jnp.float32)
        image_embedding_gradient = image_embedding_gradient + jnp.einsum('gdpq,gdqe->gdpe', coef, partner)
        piece = jnp.einsum('gdpq,gdpe->gdqe', coef, xb).astype(jnp.bfloat16)
        grad_y = grad_y + piece[partner_group_sequence][:, block_order].astype(jnp.float32)
    picture_derivative = (image_embedding_gradient - xn * lax.optimization_barrier(jnp.sum(xn * image_embedding_gradient, axis=-1, keepdims=True))) * inv_x
    text_grad = (grad_y - yn * lax.optimization_barrier(jnp.sum(yn * grad_y, axis=-1, keepdims=True))) * inv_y
    return (picture_derivative.reshape(N_GROUP, BD, E), text_grad.reshape(N_GROUP, BD, E))
```

```python
import jax
import jax.numpy as jnp
from jax import lax
from jax.sharding import PartitionSpec as P

AXES = ("dp", "group")


def routes(n_dp, n_group):
    core, first, second = [], [], []
    for d in range(n_dp):
        for g in range(n_group):
            here = d * n_group + g
            over_core = (d ^ 1) * n_group + g
            over_z = (d ^ 2) * n_group + g
            over_y = d * n_group + (g ^ 1)
            core.append((here, over_core))
            first.append((here, over_z if d & 1 else over_y))
            second.append((here, over_y if d & 1 else over_z))
    return core, first, second


def normalize(values):
    wide = values.astype(jnp.float32)
    inverse = lax.rsqrt(jnp.sum(wide * wide, axis=-1, keepdims=True) + 1e-06)
    return wide * inverse, inverse


def finish(vectors, inverse, grad):
    return (grad - vectors * jnp.sum(vectors * grad, axis=-1, keepdims=True)) * inverse


def matmul_nt(a, b):
    return lax.dot_general(a, b, (((1,), (1,)), ((), ())), preferred_element_type=jnp.float32)


def matmul_nn(a, b):
    return lax.dot_general(a, b, (((1,), (0,)), ((), ())), preferred_element_type=jnp.float32)


def matmul_tn(a, b):
    return lax.dot_general(a, b, (((0,), (0,)), ((), ())), preferred_element_type=jnp.float32)


def on_device(x, y, slot, sharpness, offset):
    core_route, first_route, second_route = routes(lax.axis_size("dp"), lax.axis_size("group"))
    on_first_core = (lax.axis_index("dp") & 1) == 0
    scale, shift = sharpness[0], offset[0]
    xn, inv_x = normalize(x[0])
    yn, inv_y = normalize(y[0])
    xb, yb = xn.astype(jnp.bfloat16), yn.astype(jnp.bfloat16)
    a_own = jnp.where(on_first_core, xb, yb)
    b_own = jnp.where(on_first_core, yb, xb)
    a_far = lax.ppermute(a_own, AXES, first_route)
    b_far = lax.ppermute(b_own, AXES, second_route)
    other = lax.ppermute(jnp.stack([a_own, b_own]), AXES, core_route)
    b_oth, a_oth = other[0], other[1]

    count = xb.shape[0]
    rows = lax.broadcasted_iota(jnp.int32, (count, count), 0)
    columns = lax.broadcasted_iota(jnp.int32, (count, count), 1)
    slots = slot[0, 0]
    positive = jnp.where(on_first_core, slots[:, None] == columns, slots[None, :] == rows)

    def coef(a, b, mask=None):
        logits = scale * matmul_nt(a, b) + shift
        if mask is None:
            return (scale * jax.nn.sigmoid(logits)).astype(jnp.bfloat16)
        sign = jnp.where(mask, 1.0, -1.0)
        return (-scale * sign * jax.nn.sigmoid(-sign * logits)).astype(jnp.bfloat16)

    c_own = coef(a_own, b_own, positive)
    c_own_oth = coef(a_own, b_oth)
    c_oth_own = coef(a_oth, b_own)
    ga_own = matmul_nn(c_own, b_own) + matmul_nn(c_own_oth, b_oth)
    gb_own = matmul_tn(c_own, a_own) + matmul_tn(c_oth_own, a_oth)

    b_far_oth = lax.ppermute(a_far, AXES, core_route)
    c_far_own = coef(a_far, b_own)
    ga_far = matmul_nn(c_far_own, b_own) + matmul_nn(coef(a_far, b_oth), b_oth)
    gb_own = gb_own + matmul_tn(c_far_own, a_far)
    ga_own = ga_own + matmul_nn(coef(a_own, b_far_oth), b_far_oth)
    ga_far = ga_far + matmul_nn(coef(a_far, b_far_oth), b_far_oth)

    a_far_oth = lax.ppermute(b_far, AXES, core_route)
    c_far_far = coef(a_far, b_far)
    ga_far = ga_far + matmul_nn(c_far_far, b_far)
    ga_back = lax.ppermute(ga_far.astype(jnp.bfloat16), AXES, first_route)
    c_own_far = coef(a_own, b_far)
    gb_far = (
        matmul_tn(c_far_far, a_far)
        + matmul_tn(c_own_far, a_own)
        + matmul_tn(coef(a_oth, b_far), a_oth)
        + matmul_tn(coef(a_far_oth, b_far), a_far_oth)
    )
    gb_back = lax.ppermute(gb_far.astype(jnp.bfloat16), AXES, second_route)
    ga_own = ga_own + matmul_nn(c_own_far, b_far)
    gb_own = gb_own + matmul_tn(coef(a_far_oth, b_own), a_far_oth)

    ga = ga_own + ga_back.astype(jnp.float32)
    gb = gb_own + gb_back.astype(jnp.float32)
    gx = jnp.where(on_first_core, ga, gb)
    gy = jnp.where(on_first_core, gb, ga)
    return finish(xn, inv_x, gx)[None], finish(yn, inv_y, gy)[None]


def solution(mesh):
    spec = P("group", "dp", None)
    return jax.shard_map(
        on_device,
        mesh=mesh,
        in_specs=(spec, spec, spec, P(), P()),
        out_specs=(spec, spec),
        check_vma=False,
    )
```

```python
import functools

import jax
import jax.numpy as jnp
from jax import lax
from jax.experimental import pallas as pl
from jax.experimental.pallas import tpu as pltpu
from jax.sharding import PartitionSpec as P

AXES = ("dp", "group")
HERE = pl.BlockSpec(memory_space=pltpu.VMEM)
AFAR = pl.BlockSpec(memory_space=pltpu.HBM)
SHORT = pl.CostEstimate(flops=1, bytes_accessed=1, transcendentals=0)
LONG = pl.CostEstimate(flops=30_000_000_000, bytes_accessed=1, transcendentals=0)
PARAMS = pltpu.CompilerParams(vmem_limit_bytes=32 * 1024 * 1024)
CHUNK = 32


def routes(n_dp, n_group):
    core, first, second = [], [], []
    for d in range(n_dp):
        for g in range(n_group):
            here = d * n_group + g
            over_core = (d ^ 1) * n_group + g
            over_z = (d ^ 2) * n_group + g
            over_y = d * n_group + (g ^ 1)
            core.append((here, over_core))
            first.append((here, over_z if d & 1 else over_y))
            second.append((here, over_y if d & 1 else over_z))
    return core, first, second


def core_of():
    return lax.axis_index("dp") & 1


def load_chunks(x_ref, y_ref, swap, raw, sems):
    copies = []
    for k in range(raw.shape[0] // CHUNK):
        at = pl.ds(k * CHUNK, CHUNK)
        from_x = pltpu.make_async_copy(x_ref.at[0, at], raw.at[at], sems.at[k])
        from_y = pltpu.make_async_copy(y_ref.at[0, at], raw.at[at], sems.at[k])
        pl.when(swap == 0)(from_x.start)
        pl.when(swap != 0)(from_y.start)
        copies.append((at, from_x))
    return copies


def unit(raw):
    wide = raw.astype(jnp.float32)
    inverse = lax.rsqrt(jnp.sum(wide * wide, axis=-1, keepdims=True) + 1e-06)
    return wide * inverse, inverse


def first_kernel(x_ref, y_ref, a_ref, raw, sems):
    for at, copy in load_chunks(x_ref, y_ref, core_of(), raw, sems):
        copy.wait()
        a_ref[at] = unit(raw[at])[0].astype(a_ref.dtype)


def second_kernel(x_ref, y_ref, a_ref, b_ref, raw, sems):
    for at, copy in load_chunks(x_ref, y_ref, 1 - core_of(), raw, sems):
        copy.wait()
        b_ref[at] = unit(raw[at])[0].astype(b_ref.dtype)


def copy_kernel(in_ref, out_ref):
    out_ref[...] = in_ref[...]


def pack_kernel(scale_ref, shift_ref, a_ref, a1_ref, b_ref, pack_ref, pair_ref):
    for k, ref in enumerate((scale_ref, shift_ref)):
        pair_ref[k] = jnp.full(pair_ref.shape[1:], ref[0])
    for k, ref in enumerate((a_ref, a1_ref, b_ref)):
        pack_ref[k] = ref[...]


def joined(refs):
    return jnp.concatenate([ref[...] for ref in refs], axis=0)


def weigh(q, keys, scale, shift, positive=None):
    logits = scale * lax.dot_general(
        q, keys, (((1,), (1,)), ((), ())), preferred_element_type=jnp.float32
    ) + shift
    if positive is None:
        return (scale * jax.nn.sigmoid(logits)).astype(jnp.bfloat16)
    wide = positive.shape[1]
    sign = jnp.where(positive, 1.0, -1.0)
    near = -scale * sign * jax.nn.sigmoid(-sign * logits[:, :wide])
    rest = scale * jax.nn.sigmoid(logits[:, wide:])
    return jnp.concatenate([near, rest], axis=1).astype(jnp.bfloat16)


def scalars_of(pair_ref):
    return pair_ref[0, 0:1, 0:1], pair_ref[1, 0:1, 0:1]


def collect(coef, key_refs, out_ref, tile=384):
    for start in range(0, out_ref.shape[-1], tile):
        at = pl.ds(start, tile)
        keys = jnp.concatenate([ref[:, at] for ref in key_refs], axis=0)
        total = jnp.dot(coef, keys, preferred_element_type=jnp.float32)
        out_ref[:, at] = total.astype(out_ref.dtype)


def partial_kernel(pair_ref, pack_ref, other_ref, b2_ref, a2_ref, out_ref):
    if a2_ref is None:
        q, keys = pack_ref.at[1], (pack_ref.at[2], other_ref.at[0], other_ref.at[1], b2_ref)
    else:
        q, keys = b2_ref, (pack_ref.at[0], pack_ref.at[1], other_ref.at[2], a2_ref)
    coef = weigh(q[...], joined(keys), *scalars_of(pair_ref))
    collect(coef, keys, out_ref)


def partial_a(pair_ref, pack_ref, other_ref, b2_ref, out_ref):
    partial_kernel(pair_ref, pack_ref, other_ref, b2_ref, None, out_ref)


def own_kernel(
    pair_ref, slot_ref, x_ref, y_ref, pack_ref, other_ref, b2_ref, a2_ref,
    ga_ref, gb_ref, an_ref, bn_ref, ia_ref, ib_ref, raw_a, raw_b, slots, sems_a, sems_b, sem,
):
    core = core_of()
    copies_a = load_chunks(x_ref, y_ref, core, raw_a, sems_a)
    copies_b = load_chunks(x_ref, y_ref, 1 - core, raw_b, sems_b)
    load = pltpu.make_async_copy(slot_ref.at[0], slots, sem)
    load.start()
    scale, shift = scalars_of(pair_ref)
    count = raw_a.shape[0]
    rows = lax.broadcasted_iota(jnp.int32, (count, count), 0)
    load.wait()
    across = jnp.broadcast_to(slots[...], (count, count))
    by_text = (across == rows).astype(jnp.float32)
    by_image = by_text.T
    first = core == 0
    mask_a = jnp.where(first, by_image, by_text) > 0.5
    mask_b = jnp.where(first, by_text, by_image) > 0.5
    a_ref, a1_ref, b_ref = (pack_ref.at[k] for k in range(3))
    b_oth, b1_ref, a_oth = (other_ref.at[k] for k in range(3))
    b_keys = (b_ref, b_oth, b1_ref, b2_ref)
    a_keys = (a_ref, a_oth, a1_ref, a2_ref)
    collect(weigh(a_ref[...], joined(b_keys), scale, shift, mask_a), b_keys, ga_ref)
    collect(weigh(b_ref[...], joined(a_keys), scale, shift, mask_b), a_keys, gb_ref)
    for copies, raw, n_ref, i_ref in (
        (copies_a, raw_a, an_ref, ia_ref), (copies_b, raw_b, bn_ref, ib_ref),
    ):
        for at, copy in copies:
            copy.wait()
            vectors, inverse = unit(raw[at])
            n_ref[at] = vectors
            i_ref[at] = jnp.broadcast_to(inverse, (CHUNK, i_ref.shape[1]))


def project(g_ref, back, n_ref, i_ref, done, here, there, sems, first):
    copies = []
    for k in range(done.shape[0] // CHUNK):
        at = pl.ds(k * CHUNK, CHUNK)
        grad = g_ref[at] + back[at].astype(jnp.float32)
        vectors = n_ref[at]
        along = jnp.sum(vectors * grad, axis=-1, keepdims=True)
        done[at] = (grad - vectors * along) * i_ref[at, 0:1]
        to_here = pltpu.make_async_copy(done.at[at], here.at[0, at], sems.at[k])
        to_there = pltpu.make_async_copy(done.at[at], there.at[0, at], sems.at[k])
        pl.when(first)(to_here.start)
        pl.when(jnp.logical_not(first))(to_there.start)
        copies.append(to_here)
    for copy in copies:
        copy.wait()


def project_a(g_ref, back, n_ref, i_ref, x_out, y_out, done, sems):
    project(g_ref, back, n_ref, i_ref, done, x_out, y_out, sems, core_of() == 0)


def project_b(g_ref, back, n_ref, i_ref, x_in, y_in, x_out, y_out, done, sems):
    project(g_ref, back, n_ref, i_ref, done, y_out, x_out, sems, core_of() == 0)


def on_device(x, y, slot, scale, shift):
    core_route, first_route, second_route = routes(lax.axis_size("dp"), lax.axis_size("group"))
    _, count, width = x.shape
    chunks = count // CHUNK
    half = jax.ShapeDtypeStruct((count, width), jnp.bfloat16)
    wide = jax.ShapeDtypeStruct((count, width), jnp.float32)
    lanes = jax.ShapeDtypeStruct((count, 128), jnp.float32)
    loads = [pltpu.VMEM((count, width), jnp.bfloat16), pltpu.SemaphoreType.DMA((chunks,))]

    pack = jax.ShapeDtypeStruct((3, count, width), jnp.bfloat16)
    call = functools.partial(pl.pallas_call, compiler_params=PARAMS, cost_estimate=SHORT)
    x, y, slot = (
        pltpu.with_memory_space_constraint(v, pltpu.HBM) for v in (x, y, slot)
    )

    a = call(
        first_kernel, out_shape=half, in_specs=[AFAR] * 2, out_specs=HERE,
        scratch_shapes=loads, name="normalize_a",
    )(x, y)
    a1 = lax.ppermute(a, AXES, first_route)
    b = call(
        second_kernel, out_shape=half, in_specs=[AFAR, AFAR, HERE], out_specs=HERE,
        scratch_shapes=loads, name="normalize_b",
    )(x, y, a)
    b2 = lax.ppermute(b, AXES, second_route)
    mine, pair = call(
        pack_kernel, out_shape=(pack, jax.ShapeDtypeStruct((2, 8, 128), jnp.float32)),
        in_specs=[pl.BlockSpec(memory_space=pltpu.SMEM)] * 2 + [HERE] * 3,
        out_specs=(HERE, HERE), name="pack",
    )(scale, shift, a, a1, b)
    other = lax.ppermute(mine, AXES, core_route)
    held = call(
        copy_kernel, out_shape=half, in_specs=[HERE], out_specs=HERE, name="copy_b2",
        cost_estimate=LONG,
    )(b2)
    a2 = lax.ppermute(held, AXES, core_route)

    part_a = call(
        partial_a, out_shape=half, in_specs=[HERE] * 4, out_specs=HERE, name="partial_a"
    )(pair, mine, other, b2)
    back_a = lax.ppermute(part_a, AXES, first_route)
    part_b = call(
        partial_kernel, out_shape=half, in_specs=[HERE] * 5, out_specs=HERE, name="partial_b"
    )(pair, mine, other, b2, a2)
    back_b = lax.ppermute(part_b, AXES, second_route)
    ga, gb, an, bn, ia, ib = call(
        own_kernel, out_shape=(wide, wide, wide, wide, lanes, lanes),
        in_specs=[HERE] + [AFAR] * 3 + [HERE] * 4, out_specs=(HERE,) * 6,
        scratch_shapes=[
            loads[0], loads[0], pltpu.VMEM((1, count), jnp.int32),
            loads[1], loads[1], pltpu.SemaphoreType.DMA,
        ],
        name="own",
    )(pair, slot, x, y, mine, other, b2, a2)
    out = jax.ShapeDtypeStruct(x.shape, jnp.float32)
    stores = [pltpu.VMEM((count, width), jnp.float32), pltpu.SemaphoreType.DMA((chunks,))]
    outs = call(
        project_a, out_shape=(out, out), in_specs=[HERE] * 4, out_specs=(AFAR, AFAR),
        scratch_shapes=stores, name="project_a",
    )(ga, back_a, an, ia)
    return call(
        project_b, out_shape=(out, out), in_specs=[HERE] * 4 + [AFAR] * 2,
        out_specs=(AFAR, AFAR), scratch_shapes=stores,
        input_output_aliases={4: 0, 5: 1}, name="project_b",
    )(gb, back_b, bn, ib, *outs)


def solution(mesh):
    spec = P("group", "dp", None)
    return jax.shard_map(
        on_device,
        mesh=mesh,
        in_specs=(spec, spec, spec, P(), P()),
        out_specs=(spec, spec),
        check_vma=False,
    )
```

```python
import functools

import jax
import jax.numpy as jnp
from jax import lax
from jax.experimental import pallas as pl
from jax.experimental.pallas import tpu as pltpu
from jax.sharding import PartitionSpec as P

AXES = ("dp", "group")
HERE = pl.BlockSpec(memory_space=pltpu.VMEM)
AFAR = pl.BlockSpec(memory_space=pltpu.HBM)
SHORT = pl.CostEstimate(flops=1, bytes_accessed=1, transcendentals=0)
LONG = pl.CostEstimate(flops=8_000_000_000, bytes_accessed=1, transcendentals=0)
PARAMS = pltpu.CompilerParams(vmem_limit_bytes=32 * 1024 * 1024)
CHUNK = 128


def routes(n_dp, n_group):
    core, first, second, crossed = [], [], [], []
    for d in range(n_dp):
        for g in range(n_group):
            here = d * n_group + g
            over_core = (d ^ 1) * n_group + g
            over_z = (d ^ 2) * n_group + g
            over_y = d * n_group + (g ^ 1)
            core.append((here, over_core))
            first.append((here, over_z if d & 1 else over_y))
            second.append((here, over_y if d & 1 else over_z))
            cross_y, cross_z = (d ^ 1) * n_group + (g ^ 1), (d ^ 3) * n_group + g
            crossed.append((here, cross_y if d & 1 else cross_z))
    return core, first, second, crossed


def core_of():
    return lax.axis_index("dp") & 1


def load_chunks(x_ref, y_ref, swap, raw, sems):
    copies = []
    for k in range(raw.shape[0] // CHUNK):
        at = pl.ds(k * CHUNK, CHUNK)
        from_x = pltpu.make_async_copy(x_ref.at[0, at], raw.at[at], sems.at[k])
        from_y = pltpu.make_async_copy(y_ref.at[0, at], raw.at[at], sems.at[k])
        pl.when(swap == 0)(from_x.start)
        pl.when(swap != 0)(from_y.start)
        copies.append((at, from_x))
    return copies


def unit(raw):
    wide = raw.astype(jnp.float32)
    inverse = lax.rsqrt(jnp.sum(wide * wide, axis=-1, keepdims=True) + 1e-06)
    return wide * inverse, inverse


def first_kernel(
    x_ref, y_ref, a_ref, raw_a, raw_b, sems_a, sems_b
):
    core = core_of()
    copies_a = load_chunks(x_ref, y_ref, core, raw_a, sems_a)
    copies_b = load_chunks(x_ref, y_ref, 1 - core, raw_b, sems_b)
    for at, copy in copies_a:
        copy.wait()
        a_ref[at] = unit(raw_a[at])[0].astype(a_ref.dtype)
    for at, copy in copies_b:
        copy.wait()


def second_kernel(raw_ref, b_ref):
    for start in range(0, b_ref.shape[0], CHUNK):
        at = pl.ds(start, CHUNK)
        b_ref[at] = unit(raw_ref[at])[0].astype(b_ref.dtype)


def keep_kernel(a2_in, b2_in, a2_out, b2_out):
    b2_out[...] = b2_in[...]
    a2_out[...] = a2_in[...]


def pack_kernel(a_ref, a1_ref, b_ref, pack_ref):
    for k, ref in enumerate((a_ref, a1_ref, b_ref)):
        pack_ref[k] = ref[...]


def joined(refs):
    return jnp.concatenate([ref[...] for ref in refs], axis=0)


def weigh(q, keys, scale, shift, positive=None):
    logits = scale * lax.dot_general(
        q, keys, (((1,), (1,)), ((), ())), preferred_element_type=jnp.float32
    ) + shift
    if positive is None:
        return (scale * jax.nn.sigmoid(logits)).astype(jnp.bfloat16)
    wide = positive.shape[1]
    sign = jnp.where(positive, 1.0, -1.0)
    near = -scale * sign * jax.nn.sigmoid(-sign * logits[:, :wide])
    rest = scale * jax.nn.sigmoid(logits[:, wide:])
    return jnp.concatenate([near, rest], axis=1).astype(jnp.bfloat16)


def scalars_of(pair_ref):
    return pair_ref[0, 0:1, 0:1], pair_ref[1, 0:1, 0:1]


def collect(coef, key_refs, out_ref, tile=1152):
    for start in range(0, out_ref.shape[-1], tile):
        at = pl.ds(start, tile)
        keys = jnp.concatenate([ref[:, at] for ref in key_refs], axis=0)
        total = jnp.dot(coef, keys, preferred_element_type=jnp.float32)
        out_ref[:, at] = total.astype(out_ref.dtype)


def contribute(pair_ref, q_ref, keys, out_ref):
    coef = weigh(q_ref[...], joined(keys), *scalars_of(pair_ref))
    collect(coef, keys, out_ref)


def partial_a(pair_ref, pack_ref, other_ref, b2_ref, out_ref):
    keys = (pack_ref.at[2], other_ref.at[0], other_ref.at[1], b2_ref)
    contribute(pair_ref, pack_ref.at[1], keys, out_ref)


def partial_b(pair_ref, pack_ref, other_ref, b2_ref, a2_ref, out_ref):
    keys = (pack_ref.at[0], pack_ref.at[1], other_ref.at[2], a2_ref)
    contribute(pair_ref, b2_ref, keys, out_ref)


def norm_kernel(raw_a, raw_b, an_ref, bn_ref, ia_ref, ib_ref):
    for raw, n_ref, i_ref in ((raw_a, an_ref, ia_ref), (raw_b, bn_ref, ib_ref)):
        vectors, inverse = unit(raw[...])
        n_ref[...] = vectors
        i_ref[...] = jnp.broadcast_to(inverse, i_ref.shape)


def own_kernel(
    pair_ref, slot_ref, pack_ref, other_ref, b2_ref, a2_ref, ga_ref, gb_ref, slots, sem
):
    load = pltpu.make_async_copy(slot_ref.at[0], slots, sem)
    load.start()
    scale, shift = scalars_of(pair_ref)
    count = b2_ref.shape[0]
    rows = lax.broadcasted_iota(jnp.int32, (count, count), 0)
    load.wait()
    across = jnp.broadcast_to(slots[...], (count, count))
    by_text = (across == rows).astype(jnp.float32)
    by_image = by_text.T
    first = core_of() == 0
    mask_a = jnp.where(first, by_image, by_text) > 0.5
    mask_b = jnp.where(first, by_text, by_image) > 0.5
    a_ref, a1_ref, b_ref = (pack_ref.at[k] for k in range(3))
    b_oth, b1_ref, a_oth = (other_ref.at[k] for k in range(3))
    b_keys = (b_ref, b_oth, b1_ref, b2_ref)
    a_keys = (a_ref, a_oth, a1_ref, a2_ref)
    collect(weigh(a_ref[...], joined(b_keys), scale, shift, mask_a), b_keys, ga_ref)
    collect(weigh(b_ref[...], joined(a_keys), scale, shift, mask_b), a_keys, gb_ref)


def project(g_ref, back, n_ref, i_ref, done, here, there, sems, first):
    copies = []
    for k in range(done.shape[0] // CHUNK):
        at = pl.ds(k * CHUNK, CHUNK)
        grad = g_ref[at] + back[at].astype(jnp.float32)
        vectors = n_ref[at]
        along = jnp.sum(vectors * grad, axis=-1, keepdims=True)
        done[at] = (grad - vectors * along) * i_ref[at, 0:1]
        to_here = pltpu.make_async_copy(done.at[at], here.at[0, at], sems.at[k])
        to_there = pltpu.make_async_copy(done.at[at], there.at[0, at], sems.at[k])
        pl.when(first)(to_here.start)
        pl.when(jnp.logical_not(first))(to_there.start)
        copies.append(to_here)
    for copy in copies:
        copy.wait()


def project_a(g_ref, back, n_ref, i_ref, x_out, y_out, done, sems):
    project(g_ref, back, n_ref, i_ref, done, x_out, y_out, sems, core_of() == 0)


def project_b(g_ref, back, n_ref, i_ref, x_in, y_in, x_out, y_out, done, sems):
    project(g_ref, back, n_ref, i_ref, done, y_out, x_out, sems, core_of() == 0)


def on_device(x, y, slot, scale, shift):
    core_route, first_route, second_route, crossed_route = routes(
        lax.axis_size("dp"), lax.axis_size("group")
    )
    _, count, width = x.shape
    chunks = count // CHUNK
    half = jax.ShapeDtypeStruct((count, width), jnp.bfloat16)
    wide = jax.ShapeDtypeStruct((count, width), jnp.float32)
    lanes = jax.ShapeDtypeStruct((count, 128), jnp.float32)
    loads = pltpu.SemaphoreType.DMA((chunks,))

    pack = jax.ShapeDtypeStruct((3, count, width), jnp.bfloat16)
    call = functools.partial(pl.pallas_call, compiler_params=PARAMS, cost_estimate=SHORT)
    x, y, slot = (pltpu.with_memory_space_constraint(v, pltpu.HBM) for v in (x, y, slot))
    pair = jnp.stack([jnp.full((8, 128), scale[0]), jnp.full((8, 128), shift[0])])

    a, raw_a, raw_b = call(
        first_kernel, out_shape=(half,) * 3, in_specs=[AFAR] * 2, out_specs=(HERE,) * 3,
        scratch_shapes=[loads] * 2, name="normalize_a",
    )(x, y)
    a1 = lax.ppermute(a, AXES, first_route)
    b = call(
        second_kernel, out_shape=half, in_specs=[HERE], out_specs=HERE, name="normalize_b"
    )(raw_b)
    b2 = lax.ppermute(b, AXES, second_route)
    a2 = lax.ppermute(b, AXES, crossed_route)
    mine = call(
        pack_kernel, out_shape=pack, in_specs=[HERE] * 3, out_specs=HERE, name="pack"
    )(a, a1, b)
    other = lax.ppermute(mine, AXES, core_route)
    a2, b2 = call(
        keep_kernel, out_shape=(half, half), in_specs=[HERE] * 2, out_specs=(HERE, HERE),
        name="keep", cost_estimate=LONG,
    )(a2, b2)
    part_a = call(
        partial_a, out_shape=half, in_specs=[HERE] * 4, out_specs=HERE, name="partial_a"
    )(pair, mine, other, b2)
    back_a = lax.ppermute(part_a, AXES, first_route)
    part_b = call(
        partial_b, out_shape=half, in_specs=[HERE] * 5, out_specs=HERE, name="partial_b"
    )(pair, mine, other, b2, a2)
    back_b = lax.ppermute(part_b, AXES, second_route)
    an, bn, ia, ib = call(
        norm_kernel, out_shape=(wide, wide, lanes, lanes), in_specs=[HERE] * 2,
        out_specs=(HERE,) * 4, name="norms",
    )(raw_a, raw_b)
    ga, gb = call(
        own_kernel, out_shape=(wide, wide), in_specs=[HERE, AFAR] + [HERE] * 4,
        out_specs=(HERE,) * 2,
        scratch_shapes=[pltpu.VMEM((1, count), jnp.int32), pltpu.SemaphoreType.DMA],
        name="own",
    )(pair, slot, mine, other, b2, a2)
    out = jax.ShapeDtypeStruct(x.shape, jnp.float32)
    stores = [pltpu.VMEM((count, width), jnp.float32), pltpu.SemaphoreType.DMA((chunks,))]
    outs = call(
        project_a, out_shape=(out, out), in_specs=[HERE] * 4, out_specs=(AFAR, AFAR),
        scratch_shapes=stores, name="project_a",
    )(ga, back_a, an, ia)
    return call(
        project_b, out_shape=(out, out), in_specs=[HERE] * 4 + [AFAR] * 2,
        out_specs=(AFAR, AFAR), scratch_shapes=stores,
        input_output_aliases={4: 0, 5: 1}, name="project_b",
    )(gb, back_b, bn, ib, *outs)


def solution(mesh):
    spec = P("group", "dp", None)
    return jax.shard_map(
        on_device,
        mesh=mesh,
        in_specs=(spec, spec, spec, P(), P()),
        out_specs=(spec, spec),
        check_vma=False,
    )
```

```python
import functools

import jax
import jax.numpy as jnp
from jax import lax
from jax.experimental import pallas as pl
from jax.experimental.pallas import tpu as pltpu
from jax.sharding import PartitionSpec as P

AXES = ("dp", "group")
HERE = pl.BlockSpec(memory_space=pltpu.VMEM)
AFAR = pl.BlockSpec(memory_space=pltpu.HBM)
SHORT = pl.CostEstimate(flops=1, bytes_accessed=1, transcendentals=0)
LONG = pl.CostEstimate(flops=8_000_000_000, bytes_accessed=1, transcendentals=0)
PARAMS = pltpu.CompilerParams(vmem_limit_bytes=32 * 1024 * 1024)
CHUNK = 128


def routes(n_dp, n_group):
    core, first, second, crossed = [], [], [], []
    for d in range(n_dp):
        for g in range(n_group):
            here = d * n_group + g
            over_core = (d ^ 1) * n_group + g
            over_z = (d ^ 2) * n_group + g
            over_y = d * n_group + (g ^ 1)
            core.append((here, over_core))
            first.append((here, over_z if d & 1 else over_y))
            second.append((here, over_y if d & 1 else over_z))
            cross_y, cross_z = (d ^ 1) * n_group + (g ^ 1), (d ^ 3) * n_group + g
            crossed.append((here, cross_y if d & 1 else cross_z))
    return core, first, second, crossed


def core_of():
    return lax.axis_index("dp") & 1


def load_chunks(x_ref, y_ref, swap, raw, sems):
    copies = []
    for k in range(raw.shape[0] // CHUNK):
        at = pl.ds(k * CHUNK, CHUNK)
        from_x = pltpu.make_async_copy(x_ref.at[0, at], raw.at[at], sems.at[k])
        from_y = pltpu.make_async_copy(y_ref.at[0, at], raw.at[at], sems.at[k])
        pl.when(swap == 0)(from_x.start)
        pl.when(swap != 0)(from_y.start)
        copies.append((at, from_x))
    return copies


def unit(raw):
    wide = raw.astype(jnp.float32)
    inverse = lax.rsqrt(jnp.sum(wide * wide, axis=-1, keepdims=True) + 1e-06)
    return wide * inverse, inverse


def first_kernel(
    x_ref, y_ref, a_ref, raw_a, raw_b, sems_a, sems_b
):
    core = core_of()
    copies_a = load_chunks(x_ref, y_ref, core, raw_a, sems_a)
    copies_b = load_chunks(x_ref, y_ref, 1 - core, raw_b, sems_b)
    for at, copy in copies_a:
        copy.wait()
        a_ref[at] = unit(raw_a[at])[0].astype(a_ref.dtype)
    for at, copy in copies_b:
        copy.wait()


def second_kernel(raw_ref, b_ref):
    for start in range(0, b_ref.shape[0], CHUNK):
        at = pl.ds(start, CHUNK)
        b_ref[at] = unit(raw_ref[at])[0].astype(b_ref.dtype)


def keep_kernel(a2_in, a2_out):
    a2_out[...] = a2_in[...]


def pack_kernel(a_ref, a1_ref, b_ref, pack_ref):
    for k, ref in enumerate((a_ref, a1_ref, b_ref)):
        pack_ref[k] = ref[...]


def joined(refs):
    return jnp.concatenate([ref[...] for ref in refs], axis=0)


def weigh(q, keys, scale, shift, positive=None):
    logits = scale * lax.dot_general(
        q, keys, (((1,), (1,)), ((), ())), preferred_element_type=jnp.float32
    ) + shift
    if positive is None:
        return (scale * jax.nn.sigmoid(logits)).astype(jnp.bfloat16)
    wide = positive.shape[1]
    sign = jnp.where(positive, 1.0, -1.0)
    near = -scale * sign * jax.nn.sigmoid(-sign * logits[:, :wide])
    rest = scale * jax.nn.sigmoid(logits[:, wide:])
    return jnp.concatenate([near, rest], axis=1).astype(jnp.bfloat16)


def scalars_of(pair_ref):
    return pair_ref[0, 0:1, 0:1], pair_ref[1, 0:1, 0:1]


def collect(coef, key_refs, out_ref, tile=1152):
    for start in range(0, out_ref.shape[-1], tile):
        at = pl.ds(start, tile)
        keys = jnp.concatenate([ref[:, at] for ref in key_refs], axis=0)
        total = jnp.dot(coef, keys, preferred_element_type=jnp.float32)
        out_ref[:, at] = total.astype(out_ref.dtype)


def contribute(pair_ref, jobs):
    scale, shift = scalars_of(pair_ref)
    coefs = [weigh(q[...], joined(keys), scale, shift) for q, keys, _, _ in jobs]
    for coef, (_, keys, more, out_ref) in zip(coefs, jobs):
        total = jnp.dot(coef, joined(keys), preferred_element_type=jnp.float32)
        if more is not None:
            total = total + more[...]
        out_ref[...] = total.astype(out_ref.dtype)


def early_kernel(pair_ref, pack_ref, b2_ref, half_a, half_b):
    jobs = (
        (pack_ref.at[1], (pack_ref.at[2], b2_ref), None, half_a),
        (b2_ref, (pack_ref.at[0], pack_ref.at[1]), None, half_b),
    )
    contribute(pair_ref, jobs)


def late_kernel(pair_ref, pack_ref, other_ref, b2_ref, a2_ref, half_a, half_b, out_a, out_b):
    jobs = (
        (pack_ref.at[1], (other_ref.at[0], other_ref.at[1]), half_a, out_a),
        (b2_ref, (other_ref.at[2], a2_ref), half_b, out_b),
    )
    contribute(pair_ref, jobs)


def norm_kernel(raw_a, raw_b, an_ref, bn_ref, ia_ref, ib_ref):
    for raw, n_ref, i_ref in ((raw_a, an_ref, ia_ref), (raw_b, bn_ref, ib_ref)):
        vectors, inverse = unit(raw[...])
        n_ref[...] = vectors
        i_ref[...] = jnp.broadcast_to(inverse, i_ref.shape)


def own_kernel(
    pair_ref, slot_ref, pack_ref, other_ref, b2_ref, a2_ref, ga_ref, gb_ref, slots, sem
):
    load = pltpu.make_async_copy(slot_ref.at[0], slots, sem)
    load.start()
    scale, shift = scalars_of(pair_ref)
    count = b2_ref.shape[0]
    rows = lax.broadcasted_iota(jnp.int32, (count, count), 0)
    load.wait()
    across = jnp.broadcast_to(slots[...], (count, count))
    by_text = (across == rows).astype(jnp.float32)
    by_image = by_text.T
    first = core_of() == 0
    mask_a = jnp.where(first, by_image, by_text) > 0.5
    mask_b = jnp.where(first, by_text, by_image) > 0.5
    a_ref, a1_ref, b_ref = (pack_ref.at[k] for k in range(3))
    b_oth, b1_ref, a_oth = (other_ref.at[k] for k in range(3))
    b_keys = (b_ref, b_oth, b1_ref, b2_ref)
    a_keys = (a_ref, a_oth, a1_ref, a2_ref)
    collect(weigh(a_ref[...], joined(b_keys), scale, shift, mask_a), b_keys, ga_ref)
    collect(weigh(b_ref[...], joined(a_keys), scale, shift, mask_b), a_keys, gb_ref)


def project(g_ref, back, n_ref, i_ref, done, here, there, sems, first):
    copies = []
    for k in range(done.shape[0] // CHUNK):
        at = pl.ds(k * CHUNK, CHUNK)
        grad = g_ref[at] + back[at].astype(jnp.float32)
        vectors = n_ref[at]
        along = jnp.sum(vectors * grad, axis=-1, keepdims=True)
        done[at] = (grad - vectors * along) * i_ref[at, 0:1]
        to_here = pltpu.make_async_copy(done.at[at], here.at[0, at], sems.at[k])
        to_there = pltpu.make_async_copy(done.at[at], there.at[0, at], sems.at[k])
        pl.when(first)(to_here.start)
        pl.when(jnp.logical_not(first))(to_there.start)
        copies.append(to_here)
    for copy in copies:
        copy.wait()


def project_a(g_ref, back, n_ref, i_ref, x_out, y_out, done, sems):
    project(g_ref, back, n_ref, i_ref, done, x_out, y_out, sems, core_of() == 0)


def project_b(g_ref, back, n_ref, i_ref, x_in, y_in, x_out, y_out, done, sems):
    project(g_ref, back, n_ref, i_ref, done, y_out, x_out, sems, core_of() == 0)


def on_device(x, y, slot, scale, shift):
    core_route, first_route, second_route, crossed_route = routes(
        lax.axis_size("dp"), lax.axis_size("group")
    )
    _, count, width = x.shape
    chunks = count // CHUNK
    half = jax.ShapeDtypeStruct((count, width), jnp.bfloat16)
    wide = jax.ShapeDtypeStruct((count, width), jnp.float32)
    lanes = jax.ShapeDtypeStruct((count, 128), jnp.float32)
    loads = pltpu.SemaphoreType.DMA((chunks,))

    pack = jax.ShapeDtypeStruct((3, count, width), jnp.bfloat16)
    call = functools.partial(pl.pallas_call, compiler_params=PARAMS, cost_estimate=SHORT)
    x, y, slot = (pltpu.with_memory_space_constraint(v, pltpu.HBM) for v in (x, y, slot))
    pair = jnp.stack([jnp.full((8, 128), scale[0]), jnp.full((8, 128), shift[0])])

    a, raw_a, raw_b = call(
        first_kernel, out_shape=(half,) * 3, in_specs=[AFAR] * 2, out_specs=(HERE,) * 3,
        scratch_shapes=[loads] * 2, name="normalize_a",
    )(x, y)
    a1 = lax.ppermute(a, AXES, first_route)
    b = call(
        second_kernel, out_shape=half, in_specs=[HERE], out_specs=HERE, name="normalize_b"
    )(raw_b)
    b2 = lax.ppermute(b, AXES, second_route)
    a2 = lax.ppermute(b, AXES, crossed_route)
    mine = call(
        pack_kernel, out_shape=pack, in_specs=[HERE] * 3, out_specs=HERE, name="pack"
    )(a, a1, b)
    other = lax.ppermute(mine, AXES, core_route)
    half_a, half_b = call(
        early_kernel, out_shape=(wide, wide), in_specs=[HERE] * 3, out_specs=(HERE, HERE),
        name="early",
    )(pair, mine, b2)
    a2 = call(
        keep_kernel, out_shape=half, in_specs=[HERE], out_specs=HERE, name="keep",
        cost_estimate=LONG,
    )(a2)
    part_a, part_b = call(
        late_kernel, out_shape=(half, half), in_specs=[HERE] * 7, out_specs=(HERE, HERE),
        name="late",
    )(pair, mine, other, b2, a2, half_a, half_b)
    back_a = lax.ppermute(part_a, AXES, first_route)
    back_b = lax.ppermute(part_b, AXES, second_route)
    an, bn, ia, ib = call(
        norm_kernel, out_shape=(wide, wide, lanes, lanes), in_specs=[HERE] * 2,
        out_specs=(HERE,) * 4, name="norms",
    )(raw_a, raw_b)
    ga, gb = call(
        own_kernel, out_shape=(wide, wide), in_specs=[HERE, AFAR] + [HERE] * 4,
        out_specs=(HERE,) * 2,
        scratch_shapes=[pltpu.VMEM((1, count), jnp.int32), pltpu.SemaphoreType.DMA],
        name="own",
    )(pair, slot, mine, other, b2, a2)
    out = jax.ShapeDtypeStruct(x.shape, jnp.float32)
    stores = [pltpu.VMEM((count, width), jnp.float32), pltpu.SemaphoreType.DMA((chunks,))]
    outs = call(
        project_a, out_shape=(out, out), in_specs=[HERE] * 4, out_specs=(AFAR, AFAR),
        scratch_shapes=stores, name="project_a",
    )(ga, back_a, an, ia)
    return call(
        project_b, out_shape=(out, out), in_specs=[HERE] * 4 + [AFAR] * 2,
        out_specs=(AFAR, AFAR), scratch_shapes=stores,
        input_output_aliases={4: 0, 5: 1}, name="project_b",
    )(gb, back_b, bn, ib, *outs)


def solution(mesh):
    spec = P("group", "dp", None)
    return jax.shard_map(
        on_device,
        mesh=mesh,
        in_specs=(spec, spec, spec, P(), P()),
        out_specs=(spec, spec),
        check_vma=False,
    )
```

```python
import functools

import jax
import jax.numpy as jnp
from jax import lax
from jax.experimental import pallas as pl
from jax.experimental.pallas import tpu as pltpu
from jax.sharding import PartitionSpec as P

AXES = ("dp", "group")
HERE = pl.BlockSpec(memory_space=pltpu.VMEM)
AFAR = pl.BlockSpec(memory_space=pltpu.HBM)
SHORT = pl.CostEstimate(flops=1, bytes_accessed=1, transcendentals=0)
LONG = pl.CostEstimate(flops=9_000_000_000, bytes_accessed=1, transcendentals=0)
FILL = pl.CostEstimate(flops=1_000_000_000, bytes_accessed=1, transcendentals=0)
PARAMS = pltpu.CompilerParams(vmem_limit_bytes=32 * 1024 * 1024)
CHUNK = 128


def routes(n_dp, n_group):
    core, first, second, crossed = [], [], [], []
    for d in range(n_dp):
        for g in range(n_group):
            here = d * n_group + g
            over_core = (d ^ 1) * n_group + g
            over_z = (d ^ 2) * n_group + g
            over_y = d * n_group + (g ^ 1)
            core.append((here, over_core))
            first.append((here, over_z if d & 1 else over_y))
            second.append((here, over_y if d & 1 else over_z))
            cross_y, cross_z = (d ^ 1) * n_group + (g ^ 1), (d ^ 3) * n_group + g
            crossed.append((here, cross_y if d & 1 else cross_z))
    return core, first, second, crossed


def core_of():
    return lax.axis_index("dp") & 1


def load_chunks(x_ref, y_ref, swap, raw, sems):
    copies = []
    for k in range(raw.shape[0] // CHUNK):
        at = pl.ds(k * CHUNK, CHUNK)
        from_x = pltpu.make_async_copy(x_ref.at[0, at], raw.at[at], sems.at[k])
        from_y = pltpu.make_async_copy(y_ref.at[0, at], raw.at[at], sems.at[k])
        pl.when(swap == 0)(from_x.start)
        pl.when(swap != 0)(from_y.start)
        copies.append((at, from_x))
    return copies


def unit(raw):
    wide = raw.astype(jnp.float32)
    inverse = lax.rsqrt(jnp.sum(wide * wide, axis=-1, keepdims=True) + 1e-06)
    return wide * inverse, inverse


def first_kernel(
    x_ref, y_ref, a_ref, raw_a, raw_b, sems_a, sems_b
):
    core = core_of()
    copies_a = load_chunks(x_ref, y_ref, core, raw_a, sems_a)
    copies_b = load_chunks(x_ref, y_ref, 1 - core, raw_b, sems_b)
    for at, copy in copies_a:
        copy.wait()
        a_ref[at] = unit(raw_a[at])[0].astype(a_ref.dtype)
    for at, copy in copies_b:
        copy.wait()


def second_kernel(raw_ref, b_ref):
    for start in range(0, b_ref.shape[0], CHUNK):
        at = pl.ds(start, CHUNK)
        b_ref[at] = unit(raw_ref[at])[0].astype(b_ref.dtype)


def pack_kernel(a_ref, a1_ref, b_ref, pack_ref):
    for k, ref in enumerate((a_ref, a1_ref, b_ref)):
        pack_ref[k] = ref[...]


def joined(refs):
    return jnp.concatenate([ref[...] for ref in refs], axis=0)


def weigh(q, keys, scale, shift, positive=None):
    logits = scale * lax.dot_general(
        q, keys, (((1,), (1,)), ((), ())), preferred_element_type=jnp.float32
    ) + shift
    if positive is None:
        return (scale * jax.nn.sigmoid(logits)).astype(jnp.bfloat16)
    wide = positive.shape[1]
    sign = jnp.where(positive, 1.0, -1.0)
    near = -scale * sign * jax.nn.sigmoid(-sign * logits[:, :wide])
    rest = scale * jax.nn.sigmoid(logits[:, wide:])
    return jnp.concatenate([near, rest], axis=1).astype(jnp.bfloat16)


def scalars_of(pair_ref):
    return pair_ref[0, 0:1, 0:1], pair_ref[1, 0:1, 0:1]


def collect(coef, key_refs, out_ref, tile=1152):
    for start in range(0, out_ref.shape[-1], tile):
        at = pl.ds(start, tile)
        keys = jnp.concatenate([ref[:, at] for ref in key_refs], axis=0)
        total = jnp.dot(coef, keys, preferred_element_type=jnp.float32)
        out_ref[:, at] = total.astype(out_ref.dtype)


def contribute(pair_ref, jobs):
    scale, shift = scalars_of(pair_ref)
    coefs = [weigh(q[...], joined(keys), scale, shift) for q, keys, _, _ in jobs]
    for coef, (_, keys, more, out_ref) in zip(coefs, jobs):
        total = jnp.dot(coef, joined(keys), preferred_element_type=jnp.float32)
        if more is not None:
            total = total + more[...]
        out_ref[...] = total.astype(out_ref.dtype)


def early_kernel(pair_ref, pack_ref, b2_ref, _, half_a, half_b):
    jobs = (
        (pack_ref.at[1], (pack_ref.at[2], b2_ref), None, half_a),
        (b2_ref, (pack_ref.at[0], pack_ref.at[1]), None, half_b),
    )
    contribute(pair_ref, jobs)


def late_a(pair_ref, pack_ref, other_ref, half_a, out_a):
    keys = (other_ref.at[0], other_ref.at[1])
    contribute(pair_ref, ((pack_ref.at[1], keys, half_a, out_a),))


def late_b(pair_ref, b2_ref, other_ref, a2_ref, half_b, out_b):
    contribute(pair_ref, ((b2_ref, (other_ref.at[2], a2_ref), half_b, out_b),))


def norm_kernel(raw_a, raw_b, an_ref, bn_ref, ia_ref, ib_ref):
    for raw, n_ref, i_ref in ((raw_a, an_ref, ia_ref), (raw_b, bn_ref, ib_ref)):
        vectors, inverse = unit(raw[...])
        n_ref[...] = vectors
        i_ref[...] = jnp.broadcast_to(inverse, i_ref.shape)


def own_kernel(
    pair_ref, slot_ref, pack_ref, other_ref, b2_ref, a2_ref, ga_ref, gb_ref, slots, sem
):
    load = pltpu.make_async_copy(slot_ref.at[0], slots, sem)
    load.start()
    scale, shift = scalars_of(pair_ref)
    count = b2_ref.shape[0]
    rows = lax.broadcasted_iota(jnp.int32, (count, count), 0)
    load.wait()
    across = jnp.broadcast_to(slots[...], (count, count))
    by_text = (across == rows).astype(jnp.float32)
    by_image = by_text.T
    first = core_of() == 0
    mask_a = jnp.where(first, by_image, by_text) > 0.5
    mask_b = jnp.where(first, by_text, by_image) > 0.5
    a_ref, a1_ref, b_ref = (pack_ref.at[k] for k in range(3))
    b_oth, b1_ref, a_oth = (other_ref.at[k] for k in range(3))
    b_keys = (b_ref, b_oth, b1_ref, b2_ref)
    a_keys = (a_ref, a_oth, a1_ref, a2_ref)
    collect(weigh(a_ref[...], joined(b_keys), scale, shift, mask_a), b_keys, ga_ref)
    collect(weigh(b_ref[...], joined(a_keys), scale, shift, mask_b), a_keys, gb_ref)


def project(g_ref, back, n_ref, i_ref, done, here, there, sems, first):
    copies = []
    for k in range(done.shape[0] // CHUNK):
        at = pl.ds(k * CHUNK, CHUNK)
        grad = g_ref[at] + back[at].astype(jnp.float32)
        vectors = n_ref[at]
        along = jnp.sum(vectors * grad, axis=-1, keepdims=True)
        done[at] = (grad - vectors * along) * i_ref[at, 0:1]
        to_here = pltpu.make_async_copy(done.at[at], here.at[0, at], sems.at[k])
        to_there = pltpu.make_async_copy(done.at[at], there.at[0, at], sems.at[k])
        pl.when(first)(to_here.start)
        pl.when(jnp.logical_not(first))(to_there.start)
        copies.append(to_here)
    for copy in copies:
        copy.wait()


def project_a(g_ref, back, n_ref, i_ref, x_out, y_out, done, sems):
    project(g_ref, back, n_ref, i_ref, done, x_out, y_out, sems, core_of() == 0)


def project_b(g_ref, back, n_ref, i_ref, x_in, y_in, x_out, y_out, done, sems):
    project(g_ref, back, n_ref, i_ref, done, y_out, x_out, sems, core_of() == 0)


def on_device(x, y, slot, scale, shift):
    core_route, first_route, second_route, crossed_route = routes(
        lax.axis_size("dp"), lax.axis_size("group")
    )
    _, count, width = x.shape
    chunks = count // CHUNK
    half = jax.ShapeDtypeStruct((count, width), jnp.bfloat16)
    wide = jax.ShapeDtypeStruct((count, width), jnp.float32)
    lanes = jax.ShapeDtypeStruct((count, 128), jnp.float32)
    loads = pltpu.SemaphoreType.DMA((chunks,))

    pack = jax.ShapeDtypeStruct((3, count, width), jnp.bfloat16)
    call = functools.partial(pl.pallas_call, compiler_params=PARAMS, cost_estimate=SHORT)
    x, y, slot = (pltpu.with_memory_space_constraint(v, pltpu.HBM) for v in (x, y, slot))
    pair = jnp.stack([jnp.full((8, 128), scale[0]), jnp.full((8, 128), shift[0])])

    a, raw_a, raw_b = call(
        first_kernel, out_shape=(half,) * 3, in_specs=[AFAR] * 2, out_specs=(HERE,) * 3,
        scratch_shapes=[loads] * 2, name="normalize_a",
    )(x, y)
    a1 = lax.ppermute(a, AXES, first_route)
    b = call(
        second_kernel, out_shape=half, in_specs=[HERE], out_specs=HERE, name="normalize_b"
    )(raw_b)
    b2 = lax.ppermute(b, AXES, second_route)
    a2 = lax.ppermute(b, AXES, crossed_route)
    mine = call(
        pack_kernel, out_shape=pack, in_specs=[HERE] * 3, out_specs=HERE, name="pack"
    )(a, a1, b)
    other = lax.ppermute(mine, AXES, core_route)
    an, bn, ia, ib = call(
        norm_kernel, out_shape=(wide, wide, lanes, lanes), in_specs=[HERE] * 2,
        out_specs=(HERE,) * 4, name="norms", cost_estimate=FILL,
    )(raw_a, raw_b)
    half_a, half_b = call(
        early_kernel, out_shape=(wide, wide), in_specs=[HERE] * 4, out_specs=(HERE, HERE),
        name="early", cost_estimate=LONG,
    )(pair, mine, b2, ia)
    part_a = call(
        late_a, out_shape=half, in_specs=[HERE] * 4, out_specs=HERE, name="late_a"
    )(pair, mine, other, half_a)
    part_b = call(
        late_b, out_shape=half, in_specs=[HERE] * 5, out_specs=HERE, name="late_b"
    )(pair, b2, other, a2, half_b)
    back_a = lax.ppermute(part_a, AXES, first_route)
    back_b = lax.ppermute(part_b, AXES, second_route)
    ga, gb = call(
        own_kernel, out_shape=(wide, wide), in_specs=[HERE, AFAR] + [HERE] * 4,
        out_specs=(HERE,) * 2,
        scratch_shapes=[pltpu.VMEM((1, count), jnp.int32), pltpu.SemaphoreType.DMA],
        name="own",
    )(pair, slot, mine, other, b2, a2)
    out = jax.ShapeDtypeStruct(x.shape, jnp.float32)
    stores = [pltpu.VMEM((count, width), jnp.float32), pltpu.SemaphoreType.DMA((chunks,))]
    outs = call(
        project_a, out_shape=(out, out), in_specs=[HERE] * 4, out_specs=(AFAR, AFAR),
        scratch_shapes=stores, name="project_a",
    )(ga, back_a, an, ia)
    return call(
        project_b, out_shape=(out, out), in_specs=[HERE] * 4 + [AFAR] * 2,
        out_specs=(AFAR, AFAR), scratch_shapes=stores,
        input_output_aliases={4: 0, 5: 1}, name="project_b",
    )(gb, back_b, bn, ib, *outs)


def solution(mesh):
    spec = P("group", "dp", None)
    return jax.shard_map(
        on_device,
        mesh=mesh,
        in_specs=(spec, spec, spec, P(), P()),
        out_specs=(spec, spec),
        check_vma=False,
    )
```

```python
import functools

import jax
import jax.numpy as jnp
from jax import lax
from jax.experimental import pallas as pl
from jax.experimental.pallas import tpu as pltpu
from jax.sharding import PartitionSpec as P

AXES = ("dp", "group")
HERE = pl.BlockSpec(memory_space=pltpu.VMEM)
AFAR = pl.BlockSpec(memory_space=pltpu.HBM)
SHORT = pl.CostEstimate(flops=1, bytes_accessed=1, transcendentals=0)
LONG = pl.CostEstimate(flops=8_000_000_000, bytes_accessed=1, transcendentals=0)
PARAMS = pltpu.CompilerParams(vmem_limit_bytes=32 * 1024 * 1024)
CHUNK = 128


def routes(n_dp, n_group):
    core, first, second, crossed = [], [], [], []
    for d in range(n_dp):
        for g in range(n_group):
            here = d * n_group + g
            over_core = (d ^ 1) * n_group + g
            over_z = (d ^ 2) * n_group + g
            over_y = d * n_group + (g ^ 1)
            core.append((here, over_core))
            first.append((here, over_y if d & 1 else over_z))
            second.append((here, over_z if d & 1 else over_y))
            cross_y, cross_z = (d ^ 1) * n_group + (g ^ 1), (d ^ 3) * n_group + g
            crossed.append((here, cross_z if d & 1 else cross_y))
    return core, first, second, crossed


def core_of():
    return 1 - (lax.axis_index("dp") & 1)


def load_chunks(x_ref, y_ref, swap, raw, sems):
    copies = []
    for k in range(raw.shape[0] // CHUNK):
        at = pl.ds(k * CHUNK, CHUNK)
        from_x = pltpu.make_async_copy(x_ref.at[0, at], raw.at[at], sems.at[k])
        from_y = pltpu.make_async_copy(y_ref.at[0, at], raw.at[at], sems.at[k])
        pl.when(swap == 0)(from_x.start)
        pl.when(swap != 0)(from_y.start)
        copies.append((at, from_x))
    return copies


def unit(raw):
    wide = raw.astype(jnp.float32)
    inverse = lax.rsqrt(jnp.sum(wide * wide, axis=-1, keepdims=True) + 1e-06)
    return wide * inverse, inverse


def first_kernel(
    x_ref, y_ref, a_ref, raw_a, raw_b, sems_a, sems_b
):
    core = core_of()
    copies_a = load_chunks(x_ref, y_ref, core, raw_a, sems_a)
    copies_b = load_chunks(x_ref, y_ref, 1 - core, raw_b, sems_b)
    for at, copy in copies_a:
        copy.wait()
        a_ref[at] = unit(raw_a[at])[0].astype(a_ref.dtype)
    for at, copy in copies_b:
        copy.wait()


def second_kernel(raw_ref, b_ref):
    for start in range(0, b_ref.shape[0], CHUNK):
        at = pl.ds(start, CHUNK)
        b_ref[at] = unit(raw_ref[at])[0].astype(b_ref.dtype)


def keep_kernel(a2_in, a2_out):
    a2_out[...] = a2_in[...]


def pack_kernel(a_ref, a1_ref, b_ref, pack_ref):
    for k, ref in enumerate((a_ref, a1_ref, b_ref)):
        pack_ref[k] = ref[...]


def joined(refs):
    return jnp.concatenate([ref[...] for ref in refs], axis=0)


def weigh(q, keys, scale, shift, positive=None):
    logits = scale * lax.dot_general(
        q, keys, (((1,), (1,)), ((), ())), preferred_element_type=jnp.float32
    ) + shift
    if positive is None:
        return (scale * jax.nn.sigmoid(logits)).astype(jnp.bfloat16)
    wide = positive.shape[1]
    sign = jnp.where(positive, 1.0, -1.0)
    near = -scale * sign * jax.nn.sigmoid(-sign * logits[:, :wide])
    rest = scale * jax.nn.sigmoid(logits[:, wide:])
    return jnp.concatenate([near, rest], axis=1).astype(jnp.bfloat16)


def scalars_of(pair_ref):
    return pair_ref[0, 0:1, 0:1], pair_ref[1, 0:1, 0:1]


def collect(coef, key_refs, out_ref, tile=1152):
    for start in range(0, out_ref.shape[-1], tile):
        at = pl.ds(start, tile)
        keys = jnp.concatenate([ref[:, at] for ref in key_refs], axis=0)
        total = jnp.dot(coef, keys, preferred_element_type=jnp.float32)
        out_ref[:, at] = total.astype(out_ref.dtype)


def contribute(pair_ref, jobs):
    scale, shift = scalars_of(pair_ref)
    coefs = [weigh(q[...], joined(keys), scale, shift) for q, keys, _, _ in jobs]
    for coef, (_, keys, more, out_ref) in zip(coefs, jobs):
        total = jnp.dot(coef, joined(keys), preferred_element_type=jnp.float32)
        if more is not None:
            total = total + more[...]
        out_ref[...] = total.astype(out_ref.dtype)


def early_kernel(pair_ref, pack_ref, b2_ref, half_a, half_b):
    jobs = (
        (pack_ref.at[1], (pack_ref.at[2], b2_ref), None, half_a),
        (b2_ref, (pack_ref.at[0], pack_ref.at[1]), None, half_b),
    )
    contribute(pair_ref, jobs)


def late_kernel(pair_ref, pack_ref, other_ref, b2_ref, a2_ref, half_a, half_b, out_a, out_b):
    jobs = (
        (pack_ref.at[1], (other_ref.at[0], other_ref.at[1]), half_a, out_a),
        (b2_ref, (other_ref.at[2], a2_ref), half_b, out_b),
    )
    contribute(pair_ref, jobs)


def norm_kernel(raw_a, raw_b, an_ref, bn_ref, ia_ref, ib_ref):
    for raw, n_ref, i_ref in ((raw_a, an_ref, ia_ref), (raw_b, bn_ref, ib_ref)):
        vectors, inverse = unit(raw[...])
        n_ref[...] = vectors
        i_ref[...] = jnp.broadcast_to(inverse, i_ref.shape)


def own_kernel(
    pair_ref, slot_ref, pack_ref, other_ref, b2_ref, a2_ref, ga_ref, gb_ref, slots, sem
):
    load = pltpu.make_async_copy(slot_ref.at[0], slots, sem)
    load.start()
    scale, shift = scalars_of(pair_ref)
    count = b2_ref.shape[0]
    rows = lax.broadcasted_iota(jnp.int32, (count, count), 0)
    load.wait()
    across = jnp.broadcast_to(slots[...], (count, count))
    by_text = (across == rows).astype(jnp.float32)
    by_image = by_text.T
    first = core_of() == 0
    mask_a = jnp.where(first, by_image, by_text) > 0.5
    mask_b = jnp.where(first, by_text, by_image) > 0.5
    a_ref, a1_ref, b_ref = (pack_ref.at[k] for k in range(3))
    b_oth, b1_ref, a_oth = (other_ref.at[k] for k in range(3))
    b_keys = (b_ref, b_oth, b1_ref, b2_ref)
    a_keys = (a_ref, a_oth, a1_ref, a2_ref)
    collect(weigh(a_ref[...], joined(b_keys), scale, shift, mask_a), b_keys, ga_ref)
    collect(weigh(b_ref[...], joined(a_keys), scale, shift, mask_b), a_keys, gb_ref)


def project(g_ref, back, n_ref, i_ref, done, here, there, sems, first):
    copies = []
    for k in range(done.shape[0] // CHUNK):
        at = pl.ds(k * CHUNK, CHUNK)
        grad = g_ref[at] + back[at].astype(jnp.float32)
        vectors = n_ref[at]
        along = jnp.sum(vectors * grad, axis=-1, keepdims=True)
        done[at] = (grad - vectors * along) * i_ref[at, 0:1]
        to_here = pltpu.make_async_copy(done.at[at], here.at[0, at], sems.at[k])
        to_there = pltpu.make_async_copy(done.at[at], there.at[0, at], sems.at[k])
        pl.when(first)(to_here.start)
        pl.when(jnp.logical_not(first))(to_there.start)
        copies.append(to_here)
    for copy in copies:
        copy.wait()


def project_a(g_ref, back, n_ref, i_ref, x_out, y_out, done, sems):
    project(g_ref, back, n_ref, i_ref, done, x_out, y_out, sems, core_of() == 0)


def project_b(g_ref, back, n_ref, i_ref, x_in, y_in, x_out, y_out, done, sems):
    project(g_ref, back, n_ref, i_ref, done, y_out, x_out, sems, core_of() == 0)


def on_device(x, y, slot, scale, shift):
    core_route, first_route, second_route, crossed_route = routes(
        lax.axis_size("dp"), lax.axis_size("group")
    )
    _, count, width = x.shape
    chunks = count // CHUNK
    half = jax.ShapeDtypeStruct((count, width), jnp.bfloat16)
    wide = jax.ShapeDtypeStruct((count, width), jnp.float32)
    lanes = jax.ShapeDtypeStruct((count, 128), jnp.float32)
    loads = pltpu.SemaphoreType.DMA((chunks,))

    pack = jax.ShapeDtypeStruct((3, count, width), jnp.bfloat16)
    call = functools.partial(pl.pallas_call, compiler_params=PARAMS, cost_estimate=SHORT)
    x, y, slot = (pltpu.with_memory_space_constraint(v, pltpu.HBM) for v in (x, y, slot))
    pair = jnp.stack([jnp.full((8, 128), scale[0]), jnp.full((8, 128), shift[0])])

    a, raw_a, raw_b = call(
        first_kernel, out_shape=(half,) * 3, in_specs=[AFAR] * 2, out_specs=(HERE,) * 3,
        scratch_shapes=[loads] * 2, name="normalize_a",
    )(x, y)
    a1 = lax.ppermute(a, AXES, first_route)
    b = call(
        second_kernel, out_shape=half, in_specs=[HERE], out_specs=HERE, name="normalize_b"
    )(raw_b)
    b2 = lax.ppermute(b, AXES, second_route)
    a2 = lax.ppermute(b, AXES, crossed_route)
    mine = call(
        pack_kernel, out_shape=pack, in_specs=[HERE] * 3, out_specs=HERE, name="pack"
    )(a, a1, b)
    other = lax.ppermute(mine, AXES, core_route)
    half_a, half_b = call(
        early_kernel, out_shape=(wide, wide), in_specs=[HERE] * 3, out_specs=(HERE, HERE),
        name="early",
    )(pair, mine, b2)
    a2 = call(
        keep_kernel, out_shape=half, in_specs=[HERE], out_specs=HERE, name="keep",
        cost_estimate=LONG,
    )(a2)
    part_a, part_b = call(
        late_kernel, out_shape=(half, half), in_specs=[HERE] * 7, out_specs=(HERE, HERE),
        name="late",
    )(pair, mine, other, b2, a2, half_a, half_b)
    back_a = lax.ppermute(part_a, AXES, first_route)
    back_b = lax.ppermute(part_b, AXES, second_route)
    an, bn, ia, ib = call(
        norm_kernel, out_shape=(wide, wide, lanes, lanes), in_specs=[HERE] * 2,
        out_specs=(HERE,) * 4, name="norms",
    )(raw_a, raw_b)
    ga, gb = call(
        own_kernel, out_shape=(wide, wide), in_specs=[HERE, AFAR] + [HERE] * 4,
        out_specs=(HERE,) * 2,
        scratch_shapes=[pltpu.VMEM((1, count), jnp.int32), pltpu.SemaphoreType.DMA],
        name="own",
    )(pair, slot, mine, other, b2, a2)
    out = jax.ShapeDtypeStruct(x.shape, jnp.float32)
    stores = [pltpu.VMEM((count, width), jnp.float32), pltpu.SemaphoreType.DMA((chunks,))]
    outs = call(
        project_a, out_shape=(out, out), in_specs=[HERE] * 4, out_specs=(AFAR, AFAR),
        scratch_shapes=stores, name="project_a",
    )(ga, back_a, an, ia)
    return call(
        project_b, out_shape=(out, out), in_specs=[HERE] * 4 + [AFAR] * 2,
        out_specs=(AFAR, AFAR), scratch_shapes=stores,
        input_output_aliases={4: 0, 5: 1}, name="project_b",
    )(gb, back_b, bn, ib, *outs)


def solution(mesh):
    spec = P("group", "dp", None)
    return jax.shard_map(
        on_device,
        mesh=mesh,
        in_specs=(spec, spec, spec, P(), P()),
        out_specs=(spec, spec),
        check_vma=False,
    )
```
